512 devices in a mesh: rows: 32 (over x, y, core), bands: 16 (over z).
Axes of the slice: x: 4, y: 4, z: 16, core: 2. Of those that a mesh axis runs over, the one named last changes fastest.
Arguments:
- psi_panels: float32 [32768, 256], P('rows', 'bands'), may hold values from -6 to 6
- rotation: float32 [256, 8000], P('rows', 'bands'), may hold values from -0.375 to 0.375
- accumulated: float32 [32768, 8000], P('rows', 'bands'), may hold values from -6 to 6
Outputs:
- rotated: float32 [32768, 8000], P('rows', 'bands')
The draws below stay inside these ranges and needn't reach their ends.
All inputs are finite; a program needn't handle non-finite values.
Results may differ from the reference program's by a relative error of at most 0.000059.
Values sent between devices are 32-bit elements; how exact they have to be, the bound alone decides.
No kernel may reach another device: no remote copies, remote signals or barrier semaphores. Data moves between devices by JAX's collectives and lax.ppermute only.
A program may use at most 64 MiB of HBM per device.

```python
import jax
import jax.numpy as jnp
from jax import lax

NB = 8000
KW = 256
MROWS = 32768


def shard_levels(key, extent, cuts, least, largest):
    def one(position, parts):
        draws = jax.random.uniform(jax.random.fold_in(jax.random.fold_in(key, 6), position), (parts,), jnp.float32, least / len(cuts), largest / len(cuts))
        return jnp.repeat(jnp.exp(draws), extent[position] // parts).reshape((-1,) + (1,) * (len(extent) - position - 1))

    loudness = one(*cuts[0])
    for cut in cuts[1:]:
        loudness = loudness * one(*cut)
    return loudness


def noise(key, shape, deviation, most, pieces=(), dtype=jnp.bfloat16):
    values = deviation * jax.random.normal(key, shape, jnp.float32)
    if pieces:
        values = values * shard_levels(key, shape, pieces, -0.22, 0.18)
    return jnp.clip(values, -most, most).astype(dtype)


def setup_inputs(seed: int = 0) -> dict:
    streams_of = jax.random.split(jax.random.key(seed), 4)
    psi_panels = noise(streams_of[0], (MROWS, KW), 1.0, 6.0, ((0, 32), (1, 16)), jnp.float32)
    rotation = noise(streams_of[1], (KW, NB), KW ** -0.5, 0.375, ((0, 32), (1, 16)), jnp.float32)
    accumulated = noise(streams_of[2], (MROWS, NB), 1.0, 6.0, ((0, 32), (1, 16)), jnp.float32)
    return dict(psi_panels=psi_panels, rotation=rotation, accumulated=accumulated)


def reference(psi_panels, rotation, accumulated):
    product = jnp.dot(psi_panels, rotation, precision=lax.Precision.HIGHEST, preferred_element_type=jnp.float32)
    return accumulated + product
```

```python
import jax
import jax.numpy as jnp
from jax import lax
from jax.experimental import pallas as pl
from jax.experimental.pallas import tpu as pltpu
from jax.sharding import PartitionSpec as P

GROUP = 4


def shifted(block, levels, by):
    return lax.ppermute(block, "bands", [(z, (z + by) % levels) for z in range(levels)])


def halves(values):
    high = values.astype(jnp.bfloat16)
    return high, (values - high.astype(jnp.float32)).astype(jnp.bfloat16)


def product(rotation, accumulated, parts, classes, levels):
    members = levels // GROUP
    width = rotation.shape[0] // levels

    def kernel(rotation_ref, accumulated_ref, *refs):
        part_refs, out_ref = refs[:-1], refs[-1]
        z = lax.axis_index("bands")
        rows = []
        for c in classes:
            own = lax.rem(z + c + levels, GROUP)
            for m in range(members):
                start = pl.multiple_of((GROUP * m + own) * width, width)
                rows.append(rotation_ref[pl.ds(start, width), :])
        rot_high, rot_low = halves(jnp.concatenate(rows, 0))
        psi_high, psi_low = halves(jnp.concatenate([ref[...] for ref in part_refs], 0))
        left = jnp.concatenate([rot_high, rot_high, rot_low], 0)
        right = jnp.concatenate([psi_high, psi_low, psi_high], 0)
        out_ref[...] = accumulated_ref[...] + lax.dot_general(
            left, right, (((0,), (0,)), ((), ())), preferred_element_type=jnp.float32
        )

    rows, columns = accumulated.shape
    return pl.pallas_call(
        kernel,
        out_shape=jax.ShapeDtypeStruct((rows, columns), jnp.float32),
        compiler_params=pltpu.CompilerParams(vmem_limit_bytes=32 << 20),
        cost_estimate=pl.CostEstimate(
            flops=6 * rows * columns * rotation.shape[0], bytes_accessed=8 * rows * columns, transcendentals=0
        ),
        name="product",
    )(rotation, accumulated, *parts)


def solution(mesh):
    levels = mesh.shape["bands"]
    planes = mesh.shape["rows"]
    stride_groups = [[z + GROUP * m for m in range(levels // GROUP)] for z in range(GROUP)]

    def local(psi_panels, rotation, accumulated):
        copies = jnp.broadcast_to(rotation[None], (planes,) + rotation.shape)
        rot_whole = lax.all_to_all(copies, "rows", 0, 0).reshape(-1, rotation.shape[1])
        own = lax.all_gather(psi_panels.T, "bands", axis=0, tiled=True, axis_index_groups=stride_groups)
        own, rot_whole = lax.optimization_barrier((own, rot_whole))
        half = own.shape[0] // 2
        above = shifted(own, levels, -1)
        below = shifted(own, levels, 1)
        far_low = shifted(own[:half], levels, -2)
        far_high = shifted(own[half:], levels, 2)
        parts = (own, above, below, far_low, far_high)
        return product(rot_whole, accumulated.T, parts, (0, 1, -1, 2), levels).T

    spec = P("rows", "bands")
    return jax.shard_map(local, mesh=mesh, in_specs=(spec, spec, spec), out_specs=spec, check_vma=False)
```

```python
import jax
import jax.numpy as jnp
from jax import lax
from jax.experimental import pallas as pl
from jax.experimental.pallas import tpu as pltpu
from jax.sharding import PartitionSpec as P

GROUP = 4
TILE = 128


def halves(values):
    high = values.astype(jnp.bfloat16)
    return high, (values - high.astype(jnp.float32)).astype(jnp.bfloat16)


def left_operand(rows):
    high, low = halves(rows)
    return jnp.concatenate([high, high, low], 0).T


def right_operand(refs):
    high, low = halves(jnp.concatenate([ref[...] for ref in refs], 0))
    return jnp.concatenate([high, low, high], 0)


def cost(flops, moved):
    return pl.CostEstimate(flops=flops, bytes_accessed=moved, transcendentals=0)


def copies(block, count):
    def kernel(block_ref, out_ref, held, in_sem, out_sems):
        load = pltpu.make_async_copy(block_ref, held, in_sem)
        load.start()
        load.wait()
        stores = [pltpu.make_async_copy(held, out_ref.at[i], out_sems.at[i]) for i in range(count)]
        for store in stores:
            store.start()
        for store in stores:
            store.wait()

    return pl.pallas_call(
        kernel,
        out_shape=jax.ShapeDtypeStruct((count,) + block.shape, block.dtype),
        in_specs=[pl.BlockSpec(memory_space=pl.ANY)],
        out_specs=pl.BlockSpec(memory_space=pl.ANY),
        scratch_shapes=[
            pltpu.VMEM(block.shape, block.dtype),
            pltpu.SemaphoreType.DMA,
            pltpu.SemaphoreType.DMA((count,)),
        ],
        compiler_params=pltpu.CompilerParams(vmem_limit_bytes=8 << 20),
        cost_estimate=cost(0, count * block.size * 4),
        name="copies",
    )(block)


def prepare(rotation, levels, cores, ahead):
    members = levels // GROUP
    width = rotation.shape[0] // levels
    piece = width // cores
    columns = rotation.shape[1]

    def kernel(rotation_ref, early_ref, late_ref):
        z = lax.axis_index("bands")

        def rows(offsets):
            found = []
            for offset in offsets:
                own = lax.rem(z + offset + levels, GROUP)
                for m in range(members):
                    for core in range(cores):
                        at = core * levels + GROUP * m + own
                        found.append(rotation_ref[pl.ds(pl.multiple_of(at * piece, piece), piece), :])
            return jnp.concatenate(found, 0)

        early_ref[...] = left_operand(rows(ahead[0]))
        late_ref[...] = left_operand(rows(ahead[1]))

    return pl.pallas_call(
        kernel,
        out_shape=[jax.ShapeDtypeStruct((columns, 3 * len(o) * members * width), jnp.bfloat16) for o in ahead],
        compiler_params=pltpu.CompilerParams(vmem_limit_bytes=8 << 20),
        cost_estimate=cost(0, 5 * rotation.size * 4),
        name="prepare",
    )(rotation)


def add_part(left, total, parts):
    def kernel(left_ref, total_ref, *refs):
        refs[-1][...] = total_ref[...] + jnp.dot(
            left_ref[...], right_operand(refs[:-1]), preferred_element_type=jnp.float32
        )

    return pl.pallas_call(
        kernel,
        out_shape=jax.ShapeDtypeStruct(total.shape, jnp.float32),
        compiler_params=pltpu.CompilerParams(vmem_limit_bytes=20 << 20),
        cost_estimate=cost(2 * left.size * total.shape[1], 8 * total.size),
        name="add_part",
    )(left, total, *parts)


def add_last(left, total, parts):
    rows, columns = total.shape
    tiles = [(at, min(TILE, rows - at)) for at in range(0, rows, TILE)]

    def kernel(left_ref, total_ref, *refs):
        out_ref, held, sems = refs[-3:]
        right = right_operand(refs[:-3])
        stores = []
        for i, (at, size) in enumerate(tiles):
            held[at : at + size, :] = total_ref[at : at + size, :] + jnp.dot(
                left_ref[at : at + size, :], right, preferred_element_type=jnp.float32
            )
            stores.append(pltpu.make_async_copy(held.at[pl.ds(at, size)], out_ref.at[pl.ds(at, size)], sems.at[i]))
            stores[-1].start()
        for store in stores:
            store.wait()

    whole = pl.BlockSpec(memory_space=pltpu.VMEM)
    return pl.pallas_call(
        kernel,
        out_shape=jax.ShapeDtypeStruct(total.shape, jnp.float32),
        in_specs=[whole] * (2 + len(parts)),
        out_specs=pl.BlockSpec(memory_space=pl.ANY),
        scratch_shapes=[pltpu.VMEM((rows, columns), jnp.float32), pltpu.SemaphoreType.DMA((len(tiles),))],
        compiler_params=pltpu.CompilerParams(vmem_limit_bytes=20 << 20),
        cost_estimate=cost(2 * left.size * columns, 8 * total.size),
        name="add_last",
    )(left, total, *parts)


def solution(mesh):
    levels, planes = mesh.shape["bands"], mesh.shape["rows"]
    cores = 2
    chips = planes // cores
    same_core = [[cores * chip + core for chip in range(chips)] for core in range(cores)]
    same_chip = [[cores * chip + core for core in range(cores)] for chip in range(chips)]
    same_class = [[z + GROUP * m for m in range(levels // GROUP)] for z in range(GROUP)]

    def sent(block, by):
        pairs = [(i * levels + z, i * levels + (z + by(z)) % levels) for i in range(planes) for z in range(levels)]
        return lax.ppermute(block, ("rows", "bands"), pairs)

    def local(psi_panels, rotation, accumulated):
        spread = lax.all_to_all(copies(rotation, chips), "rows", 0, 0, axis_index_groups=same_core)
        spread = spread.reshape(-1, rotation.shape[1])
        own = lax.all_gather(psi_panels.T, "bands", axis=0, tiled=True, axis_index_groups=same_class)
        own, spread = lax.optimization_barrier((own, spread))
        above = sent(own, lambda z: -1)
        below = sent(own, lambda z: 1)
        across = sent(own, lambda z: 2 if z % 2 == 0 else -2)
        rot_whole = lax.all_gather(spread, "rows", axis=0, tiled=True, axis_index_groups=same_chip)
        early, late = prepare(rot_whole, levels, cores, ((0, 1, -1), (2,)))
        total = add_part(early, accumulated.T, (own, above, below))
        return add_last(late, total, (across,)).T

    spec = P("rows", "bands")
    return jax.shard_map(local, mesh=mesh, in_specs=(spec, spec, spec), out_specs=spec, check_vma=False)
```

```python
import jax
import jax.numpy as jnp
from jax import lax
from jax.experimental import pallas as pl
from jax.experimental.pallas import tpu as pltpu
from jax.sharding import PartitionSpec as P

TILE = 128
LONG = 10**11

HELD = ((0, 0), (3, -3), (4, -4), (7, -7))
FROM = ((0, 0), (1, 1), (-1, -1), (2, -2))


def halves(values):
    high = values.astype(jnp.bfloat16)
    return high, (values - high.astype(jnp.float32)).astype(jnp.bfloat16)


def left_operand(rows):
    high, low = halves(rows)
    return jnp.concatenate([high, high, low], 0).T


def right_operand(refs):
    high, low = halves(jnp.concatenate([ref[...] for ref in refs], 0))
    return jnp.concatenate([high, low, high], 0)


def cost(flops, moved):
    return pl.CostEstimate(flops=flops, bytes_accessed=moved, transcendentals=0)


def copies(block, count):
    def kernel(block_ref, out_ref, held, in_sem, out_sems):
        load = pltpu.make_async_copy(block_ref, held, in_sem)
        load.start()
        load.wait()
        stores = [pltpu.make_async_copy(held, out_ref.at[i], out_sems.at[i]) for i in range(count)]
        for store in stores:
            store.start()
        for store in stores:
            store.wait()

    return pl.pallas_call(
        kernel,
        out_shape=jax.ShapeDtypeStruct((count,) + block.shape, block.dtype),
        in_specs=[pl.BlockSpec(memory_space=pl.ANY)],
        out_specs=pl.BlockSpec(memory_space=pl.ANY),
        scratch_shapes=[
            pltpu.VMEM(block.shape, block.dtype),
            pltpu.SemaphoreType.DMA,
            pltpu.SemaphoreType.DMA((count,)),
        ],
        compiler_params=pltpu.CompilerParams(vmem_limit_bytes=8 << 20),
        cost_estimate=cost(LONG, count * block.size * 4),
        name="copies",
    )(block)


def stacked(blocks):
    rows, columns = blocks[0].shape

    def kernel(*refs):
        for i, ref in enumerate(refs[:-1]):
            refs[-1][rows * i : rows * (i + 1), :] = ref[...]

    return pl.pallas_call(
        kernel,
        out_shape=jax.ShapeDtypeStruct((rows * len(blocks), columns), blocks[0].dtype),
        compiler_params=pltpu.CompilerParams(vmem_limit_bytes=8 << 20),
        cost_estimate=cost(LONG, 8 * rows * columns * len(blocks)),
        name="stacked",
    )(*blocks)


def prepare(rotation, levels, cores, sources):
    width = rotation.shape[0] // levels
    piece = width // cores
    columns = rotation.shape[1]

    def kernel(rotation_ref, early_ref, late_ref):
        z = lax.axis_index("bands")

        def moved(level, offsets):
            even, odd = offsets
            return lax.rem(level + jnp.where(lax.rem(level, 2) == 0, even, odd) + levels, levels)

        def rows(part):
            found = []
            for source in part:
                holder = moved(z, source)
                for offsets in HELD:
                    level = moved(holder, offsets)
                    for core in range(cores):
                        at = pl.multiple_of((core * levels + level) * piece, piece)
                        found.append(rotation_ref[pl.ds(at, piece), :])
            return jnp.concatenate(found, 0)

        early_ref[...] = left_operand(rows(sources[0]))
        late_ref[...] = left_operand(rows(sources[1]))

    return pl.pallas_call(
        kernel,
        out_shape=[
            jax.ShapeDtypeStruct((columns, 3 * len(part) * len(HELD) * width), jnp.bfloat16) for part in sources
        ],
        compiler_params=pltpu.CompilerParams(vmem_limit_bytes=8 << 20),
        cost_estimate=cost(0, 5 * rotation.size * 4),
        name="prepare",
    )(rotation)


def add_part(left, total, parts):
    def kernel(left_ref, total_ref, *refs):
        refs[-1][...] = total_ref[...] + jnp.dot(
            left_ref[...], right_operand(refs[:-1]), preferred_element_type=jnp.float32
        )

    return pl.pallas_call(
        kernel,
        out_shape=jax.ShapeDtypeStruct(total.shape, jnp.float32),
        compiler_params=pltpu.CompilerParams(vmem_limit_bytes=20 << 20),
        cost_estimate=cost(2 * left.size * total.shape[1], 8 * total.size),
        name="add_part",
    )(left, total, *parts)


def add_last(left, total, parts):
    rows, columns = total.shape
    tiles = [(at, min(TILE, rows - at)) for at in range(0, rows, TILE)]

    def kernel(left_ref, total_ref, *refs):
        out_ref, held, sems = refs[-3:]
        right = right_operand(refs[:-3])
        stores = []
        for i, (at, size) in enumerate(tiles):
            held[at : at + size, :] = total_ref[at : at + size, :] + jnp.dot(
                left_ref[at : at + size, :], right, preferred_element_type=jnp.float32
            )
            stores.append(pltpu.make_async_copy(held.at[pl.ds(at, size)], out_ref.at[pl.ds(at, size)], sems.at[i]))
            stores[-1].start()
        for store in stores:
            store.wait()

    whole = pl.BlockSpec(memory_space=pltpu.VMEM)
    return pl.pallas_call(
        kernel,
        out_shape=jax.ShapeDtypeStruct(total.shape, jnp.float32),
        in_specs=[whole] * (2 + len(parts)),
        out_specs=pl.BlockSpec(memory_space=pl.ANY),
        scratch_shapes=[pltpu.VMEM((rows, columns), jnp.float32), pltpu.SemaphoreType.DMA((len(tiles),))],
        compiler_params=pltpu.CompilerParams(vmem_limit_bytes=20 << 20),
        cost_estimate=cost(2 * left.size * columns, 8 * total.size),
        name="add_last",
    )(left, total, *parts)


def solution(mesh):
    levels, planes = mesh.shape["bands"], mesh.shape["rows"]
    cores = 2
    chips = planes // cores
    same_core = [[cores * chip + core for chip in range(chips)] for core in range(cores)]
    same_chip = [[cores * chip + core for core in range(cores)] for chip in range(chips)]

    def fetched(block, offsets):
        pairs = [
            (i * levels + (z + offsets[z % 2]) % levels, i * levels + z) for i in range(planes) for z in range(levels)
        ]
        return lax.ppermute(block, ("rows", "bands"), pairs)

    def local(psi_panels, rotation, accumulated):
        spread = lax.all_to_all(copies(rotation, chips), "rows", 0, 0, axis_index_groups=same_core)
        spread = spread.reshape(-1, rotation.shape[1])
        psi = psi_panels.T
        own = stacked([psi] + [fetched(psi, offsets) for offsets in HELD[1:]])
        above, below, across = [fetched(own, offsets) for offsets in FROM[1:]]
        rot_whole = lax.all_gather(spread, "rows", axis=0, tiled=True, axis_index_groups=same_chip)
        early, late = prepare(rot_whole, levels, cores, (FROM[:3], FROM[3:]))
        total = add_part(early, accumulated.T, (own, above, below))
        return add_last(late, total, (across,)).T

    spec = P("rows", "bands")
    return jax.shard_map(local, mesh=mesh, in_specs=(spec, spec, spec), out_specs=spec, check_vma=False)
```

```python
import jax
import jax.numpy as jnp
from jax import lax
from jax.experimental import pallas as pl
from jax.experimental.pallas import tpu as pltpu
from jax.sharding import PartitionSpec as P

TILE = 128
LONG = 10**11

PAIR = 3
HOP = (4, -4)
HELD = ((0, -3), (3, 0), (4, -7), (7, -4))
FROM = ((0, 0), (-1, -1), (2, -2), (1, 1))


def halves(values):
    high = values.astype(jnp.bfloat16)
    return high, (values - high.astype(jnp.float32)).astype(jnp.bfloat16)


def left_operand(rows):
    high, low = halves(rows)
    return jnp.concatenate([high, high, low], 0).T


def right_operand(refs):
    high, low = halves(jnp.concatenate([ref[...] for ref in refs], 0))
    return jnp.concatenate([high, low, high], 0)


def cost(flops, moved):
    return pl.CostEstimate(flops=flops, bytes_accessed=moved, transcendentals=0)


def copies(block, count):
    def kernel(block_ref, out_ref, sems):
        stores = [pltpu.make_async_copy(block_ref, out_ref.at[i], sems.at[i]) for i in range(count)]
        for store in stores:
            store.start()
        for store in stores:
            store.wait()

    return pl.pallas_call(
        kernel,
        out_shape=jax.ShapeDtypeStruct((count,) + block.shape, block.dtype),
        in_specs=[pl.BlockSpec(memory_space=pltpu.VMEM)],
        out_specs=pl.BlockSpec(memory_space=pl.ANY),
        scratch_shapes=[pltpu.SemaphoreType.DMA((count,))],
        compiler_params=pltpu.CompilerParams(vmem_limit_bytes=8 << 20),
        cost_estimate=cost(LONG, count * block.size * 4),
        name="copies",
    )(block)


def stacked(blocks):
    rows, columns = blocks[0].shape

    def kernel(*refs):
        for i, ref in enumerate(refs[:-1]):
            refs[-1][rows * i : rows * (i + 1), :] = ref[...]

    return pl.pallas_call(
        kernel,
        out_shape=jax.ShapeDtypeStruct((rows * len(blocks), columns), blocks[0].dtype),
        compiler_params=pltpu.CompilerParams(vmem_limit_bytes=8 << 20),
        cost_estimate=cost(LONG, 8 * rows * columns * len(blocks)),
        name="stacked",
    )(*blocks)


def prepare(rotation, levels, cores, sources):
    width = rotation.shape[0] // levels
    piece = width // cores
    columns = rotation.shape[1]

    def kernel(rotation_ref, early_ref, late_ref):
        z = lax.axis_index("bands")

        def moved(level, offsets):
            even, odd = offsets
            return lax.rem(level + jnp.where(lax.rem(level, 2) == 0, even, odd) + levels, levels)

        def rows(part):
            found = []
            for source in part:
                holder = moved(z, source)
                for offsets in HELD:
                    level = moved(holder, offsets)
                    for core in range(cores):
                        at = pl.multiple_of((core * levels + level) * piece, piece)
                        found.append(rotation_ref[pl.ds(at, piece), :])
            return jnp.concatenate(found, 0)

        early_ref[...] = left_operand(rows(sources[0]))
        late_ref[...] = left_operand(rows(sources[1]))

    return pl.pallas_call(
        kernel,
        out_shape=[
            jax.ShapeDtypeStruct((columns, 3 * len(part) * len(HELD) * width), jnp.bfloat16) for part in sources
        ],
        compiler_params=pltpu.CompilerParams(vmem_limit_bytes=8 << 20),
        cost_estimate=cost(0, 5 * rotation.size * 4),
        name="prepare",
    )(rotation)


def add_part(left, total, parts):
    def kernel(left_ref, total_ref, *refs):
        refs[-1][...] = total_ref[...] + jnp.dot(
            left_ref[...], right_operand(refs[:-1]), preferred_element_type=jnp.float32
        )

    return pl.pallas_call(
        kernel,
        out_shape=jax.ShapeDtypeStruct(total.shape, jnp.float32),
        compiler_params=pltpu.CompilerParams(vmem_limit_bytes=20 << 20),
        cost_estimate=cost(2 * left.size * total.shape[1], 8 * total.size),
        name="add_part",
    )(left, total, *parts)


def add_last(left, total, parts):
    rows, columns = total.shape
    tiles = [(at, min(TILE, rows - at)) for at in range(0, rows, TILE)]

    def kernel(left_ref, total_ref, *refs):
        out_ref, held, sems = refs[-3:]
        right = right_operand(refs[:-3])
        stores = []
        for i, (at, size) in enumerate(tiles):
            held[at : at + size, :] = total_ref[at : at + size, :] + jnp.dot(
                left_ref[at : at + size, :], right, preferred_element_type=jnp.float32
            )
            stores.append(pltpu.make_async_copy(held.at[pl.ds(at, size)], out_ref.at[pl.ds(at, size)], sems.at[i]))
            stores[-1].start()
        for store in stores:
            store.wait()

    whole = pl.BlockSpec(memory_space=pltpu.VMEM)
    return pl.pallas_call(
        kernel,
        out_shape=jax.ShapeDtypeStruct(total.shape, jnp.float32),
        in_specs=[whole] * (2 + len(parts)),
        out_specs=pl.BlockSpec(memory_space=pl.ANY),
        scratch_shapes=[pltpu.VMEM((rows, columns), jnp.float32), pltpu.SemaphoreType.DMA((len(tiles),))],
        compiler_params=pltpu.CompilerParams(vmem_limit_bytes=20 << 20),
        cost_estimate=cost(2 * left.size * columns, 8 * total.size),
        name="add_last",
    )(left, total, *parts)


def solution(mesh):
    levels, planes = mesh.shape["bands"], mesh.shape["rows"]
    cores = 2
    chips = planes // cores
    same_core = [[cores * chip + core for chip in range(chips)] for core in range(cores)]
    same_chip = [[cores * chip + core for core in range(cores)] for chip in range(chips)]

    def fetched(block, offsets):
        pairs = [
            (i * levels + (z + offsets[z % 2]) % levels, i * levels + z) for i in range(planes) for z in range(levels)
        ]
        return lax.ppermute(block, ("rows", "bands"), pairs)

    def local(psi_panels, rotation, accumulated):
        spread = lax.all_to_all(copies(rotation, chips), "rows", 0, 0, axis_index_groups=same_core)
        spread = spread.reshape(-1, rotation.shape[1])
        pairs = [[z, (z + PAIR) % levels] for z in range(0, levels, 2)]
        couple = lax.all_gather(psi_panels.T, "bands", axis=0, tiled=True, axis_index_groups=pairs)
        own = stacked([couple, fetched(couple, HOP)])
        below, across, above = [fetched(own, offsets) for offsets in FROM[1:]]
        rot_whole = lax.all_gather(spread, "rows", axis=0, tiled=True, axis_index_groups=same_chip)
        early, late = prepare(rot_whole, levels, cores, (FROM[:3], FROM[3:]))
        total = add_part(early, accumulated.T, (own, below, across))
        return add_last(late, total, (above,)).T

    spec = P("rows", "bands")
    return jax.shard_map(local, mesh=mesh, in_specs=(spec, spec, spec), out_specs=spec, check_vma=False)
```

```python
import jax
import jax.numpy as jnp
from jax import lax
from jax.experimental import pallas as pl
from jax.experimental.pallas import tpu as pltpu
from jax.sharding import PartitionSpec as P

TILE = 128
LONG = 10**11

PAIR = 3
HOP = (-4, 4)
HELD = ((-3, 0), (0, 3), (-7, 4), (-4, 7))
FROM = ((0, 0), (-1, -1), (-2, 2), (1, 1))


def halves(values):
    high = values.astype(jnp.bfloat16)
    return high, (values - high.astype(jnp.float32)).astype(jnp.bfloat16)


def left_operand(rows):
    high, low = halves(rows)
    return jnp.concatenate([high, high, low], 0).T


def right_operand(refs):
    high, low = halves(jnp.concatenate([ref[...] for ref in refs], 0))
    return jnp.concatenate([high, low, high], 0)


def cost(flops, moved):
    return pl.CostEstimate(flops=flops, bytes_accessed=moved, transcendentals=0)


def stacked(blocks):
    rows, columns = blocks[0].shape

    def kernel(*refs):
        for i, ref in enumerate(refs[:-1]):
            refs[-1][rows * i : rows * (i + 1), :] = ref[...]

    return pl.pallas_call(
        kernel,
        out_shape=jax.ShapeDtypeStruct((rows * len(blocks), columns), blocks[0].dtype),
        compiler_params=pltpu.CompilerParams(vmem_limit_bytes=8 << 20),
        cost_estimate=cost(LONG, 8 * rows * columns * len(blocks)),
        name="stacked",
    )(*blocks)


def prepare(rotation, levels, cores, sources):
    width = rotation.shape[0] // levels
    piece = width // cores
    columns = rotation.shape[1]

    def kernel(rotation_ref, early_ref, late_ref):
        z = lax.axis_index("bands")

        def moved(level, offsets):
            even, odd = offsets
            return lax.rem(level + jnp.where(lax.rem(level, 2) == 0, even, odd) + levels, levels)

        def rows(part):
            found = []
            for source in part:
                holder = moved(z, source)
                for offsets in HELD:
                    level = moved(holder, offsets)
                    for core in range(cores):
                        at = pl.multiple_of((core * levels + level) * piece, piece)
                        found.append(rotation_ref[pl.ds(at, piece), :])
            return jnp.concatenate(found, 0)

        early_ref[...] = left_operand(rows(sources[0]))
        late_ref[...] = left_operand(rows(sources[1]))

    return pl.pallas_call(
        kernel,
        out_shape=[
            jax.ShapeDtypeStruct((columns, 3 * len(part) * len(HELD) * width), jnp.bfloat16) for part in sources
        ],
        compiler_params=pltpu.CompilerParams(vmem_limit_bytes=8 << 20),
        cost_estimate=cost(0, 5 * rotation.size * 4),
        name="prepare",
    )(rotation)


def add_part(left, total, parts):
    def kernel(left_ref, total_ref, *refs):
        refs[-1][...] = total_ref[...] + jnp.dot(
            left_ref[...], right_operand(refs[:-1]), preferred_element_type=jnp.float32
        )

    return pl.pallas_call(
        kernel,
        out_shape=jax.ShapeDtypeStruct(total.shape, jnp.float32),
        compiler_params=pltpu.CompilerParams(vmem_limit_bytes=20 << 20),
        cost_estimate=cost(2 * left.size * total.shape[1], 8 * total.size),
        name="add_part",
    )(left, total, *parts)


def add_last(left, total, parts):
    rows, columns = total.shape
    tiles = [(at, min(TILE, rows - at)) for at in range(0, rows, TILE)]

    def kernel(left_ref, total_ref, *refs):
        out_ref, held, sems = refs[-3:]
        right = right_operand(refs[:-3])
        stores = []
        for i, (at, size) in enumerate(tiles):
            held[at : at + size, :] = total_ref[at : at + size, :] + jnp.dot(
                left_ref[at : at + size, :], right, preferred_element_type=jnp.float32
            )
            stores.append(pltpu.make_async_copy(held.at[pl.ds(at, size)], out_ref.at[pl.ds(at, size)], sems.at[i]))
            stores[-1].start()
        for store in stores:
            store.wait()

    whole = pl.BlockSpec(memory_space=pltpu.VMEM)
    return pl.pallas_call(
        kernel,
        out_shape=jax.ShapeDtypeStruct(total.shape, jnp.float32),
        in_specs=[whole] * (2 + len(parts)),
        out_specs=pl.BlockSpec(memory_space=pl.ANY),
        scratch_shapes=[pltpu.VMEM((rows, columns), jnp.float32), pltpu.SemaphoreType.DMA((len(tiles),))],
        compiler_params=pltpu.CompilerParams(vmem_limit_bytes=20 << 20),
        cost_estimate=cost(2 * left.size * columns, 8 * total.size),
        name="add_last",
    )(left, total, *parts)


def solution(mesh):
    levels, planes = mesh.shape["bands"], mesh.shape["rows"]
    cores = 2
    chips = planes // cores
    same_core = [[cores * chip + core for chip in range(chips)] for core in range(cores)]
    same_chip = [[cores * chip + core for core in range(cores)] for chip in range(chips)]

    def fetched(block, offsets):
        pairs = [
            (i * levels + (z + offsets[z % 2]) % levels, i * levels + z) for i in range(planes) for z in range(levels)
        ]
        return lax.ppermute(block, ("rows", "bands"), pairs)

    def local(psi_panels, rotation, accumulated):
        copies = jnp.broadcast_to(rotation[None], (chips,) + rotation.shape)
        spread = lax.all_to_all(copies, "rows", 0, 0, axis_index_groups=same_core)
        spread = spread.reshape(-1, rotation.shape[1])
        pairs = [[z, (z + PAIR) % levels] for z in range(1, levels, 2)]
        couple = lax.all_gather(psi_panels.T, "bands", axis=0, tiled=True, axis_index_groups=pairs)
        own = stacked([couple, fetched(couple, HOP)])
        below, across, above = [fetched(own, offsets) for offsets in FROM[1:]]
        rot_whole = lax.all_gather(spread, "rows", axis=0, tiled=True, axis_index_groups=same_chip)
        early, late = prepare(rot_whole, levels, cores, (FROM[:3], FROM[3:]))
        total = add_part(early, accumulated.T, (own, below, across))
        return add_last(late, total, (above,)).T

    spec = P("rows", "bands")
    return jax.shard_map(local, mesh=mesh, in_specs=(spec, spec, spec), out_specs=spec, check_vma=False)
```

```python
import jax
import jax.numpy as jnp
from jax import lax
from jax.experimental import pallas as pl
from jax.experimental.pallas import tpu as pltpu
from jax.sharding import PartitionSpec as P

TILE = 128
LONG = 10**11

PAIR = 3
HOP = (-4, 4)
HELD = ((-3, 0), (0, 3), (-7, 4), (-4, 7))
FROM = ((0, 0), (-1, 1), (-2, 2), (1, -1))


def halves(values):
    high = values.astype(jnp.bfloat16)
    return high, (values - high.astype(jnp.float32)).astype(jnp.bfloat16)


def left_operand(rows):
    high, low = halves(rows)
    return jnp.concatenate([high, high, low], 0).T


def right_operand(refs):
    high, low = halves(jnp.concatenate([ref[...] for ref in refs], 0))
    return jnp.concatenate([high, low, high], 0)


def cost(flops, moved):
    return pl.CostEstimate(flops=flops, bytes_accessed=moved, transcendentals=0)


def stacked(blocks):
    rows, columns = blocks[0].shape

    def kernel(*refs):
        for i, ref in enumerate(refs[:-1]):
            refs[-1][rows * i : rows * (i + 1), :] = ref[...]

    return pl.pallas_call(
        kernel,
        out_shape=jax.ShapeDtypeStruct((rows * len(blocks), columns), blocks[0].dtype),
        compiler_params=pltpu.CompilerParams(vmem_limit_bytes=8 << 20),
        cost_estimate=cost(LONG, 8 * rows * columns * len(blocks)),
        name="stacked",
    )(*blocks)


def prepare(rotation, levels, cores, sources):
    width = rotation.shape[0] // levels
    piece = width // cores
    columns = rotation.shape[1]

    def kernel(rotation_ref, early_ref, late_ref):
        z = lax.axis_index("bands")

        def moved(level, offsets):
            even, odd = offsets
            return lax.rem(level + jnp.where(lax.rem(level, 2) == 0, even, odd) + levels, levels)

        def rows(part):
            found = []
            for source in part:
                holder = moved(z, source)
                for offsets in HELD:
                    level = moved(holder, offsets)
                    for core in range(cores):
                        at = pl.multiple_of((core * levels + level) * piece, piece)
                        found.append(rotation_ref[pl.ds(at, piece), :])
            return jnp.concatenate(found, 0)

        early_ref[...] = left_operand(rows(sources[0]))
        late_ref[...] = left_operand(rows(sources[1]))

    return pl.pallas_call(
        kernel,
        out_shape=[
            jax.ShapeDtypeStruct((columns, 3 * len(part) * len(HELD) * width), jnp.bfloat16) for part in sources
        ],
        compiler_params=pltpu.CompilerParams(vmem_limit_bytes=8 << 20),
        cost_estimate=cost(0, 5 * rotation.size * 4),
        name="prepare",
    )(rotation)


def add_part(left, total, parts):
    def kernel(left_ref, total_ref, *refs):
        refs[-1][...] = total_ref[...] + jnp.dot(
            left_ref[...], right_operand(refs[:-1]), preferred_element_type=jnp.float32
        )

    return pl.pallas_call(
        kernel,
        out_shape=jax.ShapeDtypeStruct(total.shape, jnp.float32),
        compiler_params=pltpu.CompilerParams(vmem_limit_bytes=20 << 20),
        cost_estimate=cost(2 * left.size * total.shape[1], 8 * total.size),
        name="add_part",
    )(left, total, *parts)


def add_last(left, total, parts):
    rows, columns = total.shape
    tiles = [(at, min(TILE, rows - at)) for at in range(0, rows, TILE)]

    def kernel(left_ref, total_ref, *refs):
        out_ref, held, sems = refs[-3:]
        right = right_operand(refs[:-3])
        stores = []
        for i, (at, size) in enumerate(tiles):
            held[at : at + size, :] = total_ref[at : at + size, :] + jnp.dot(
                left_ref[at : at + size, :], right, preferred_element_type=jnp.float32
            )
            stores.append(pltpu.make_async_copy(held.at[pl.ds(at, size)], out_ref.at[pl.ds(at, size)], sems.at[i]))
            stores[-1].start()
        for store in stores:
            store.wait()

    whole = pl.BlockSpec(memory_space=pltpu.VMEM)
    return pl.pallas_call(
        kernel,
        out_shape=jax.ShapeDtypeStruct(total.shape, jnp.float32),
        in_specs=[whole] * (2 + len(parts)),
        out_specs=pl.BlockSpec(memory_space=pl.ANY),
        scratch_shapes=[pltpu.VMEM((rows, columns), jnp.float32), pltpu.SemaphoreType.DMA((len(tiles),))],
        compiler_params=pltpu.CompilerParams(vmem_limit_bytes=20 << 20),
        cost_estimate=cost(2 * left.size * columns, 8 * total.size),
        name="add_last",
    )(left, total, *parts)


def solution(mesh):
    levels, planes = mesh.shape["bands"], mesh.shape["rows"]
    cores = 2
    chips = planes // cores
    same_core = [[cores * chip + core for chip in range(chips)] for core in range(cores)]
    same_chip = [[cores * chip + core for core in range(cores)] for chip in range(chips)]

    def fetched(block, offsets):
        pairs = [
            (i * levels + (z + offsets[z % 2]) % levels, i * levels + z) for i in range(planes) for z in range(levels)
        ]
        return lax.ppermute(block, ("rows", "bands"), pairs)

    def local(psi_panels, rotation, accumulated):
        copies = jnp.broadcast_to(rotation[None], (chips,) + rotation.shape)
        spread = lax.all_to_all(copies, "rows", 0, 0, axis_index_groups=same_core)
        spread = spread.reshape(-1, rotation.shape[1])
        pairs = [[z, (z + PAIR) % levels] for z in range(1, levels, 2)]
        couple = lax.all_gather(psi_panels.T, "bands", axis=0, tiled=True, axis_index_groups=pairs)
        own = stacked([couple, fetched(couple, HOP)])
        first, across, second = [fetched(own, offsets) for offsets in FROM[1:]]
        rot_whole = lax.all_gather(spread, "rows", axis=0, tiled=True, axis_index_groups=same_chip)
        early, late = prepare(rot_whole, levels, cores, (FROM[:3], FROM[3:]))
        total = add_part(early, accumulated.T, (own, first, across))
        return add_last(late, total, (second,)).T

    spec = P("rows", "bands")
    return jax.shard_map(local, mesh=mesh, in_specs=(spec, spec, spec), out_specs=spec, check_vma=False)
```

```python
import jax
import jax.numpy as jnp
from jax import lax
from jax.experimental import pallas as pl
from jax.experimental.pallas import tpu as pltpu
from jax.sharding import PartitionSpec as P

TILE = 128
LONG = 3 * 10**9

PAIR = 3
HOP = (-4, 4)
HELD = ((-3, 0), (0, 3), (-7, 4), (-4, 7))
FROM = ((0, 0), (-1, -1), (-2, 2), (1, 1))


def halves(values):
    high = values.astype(jnp.bfloat16)
    return high, (values - high.astype(jnp.float32)).astype(jnp.bfloat16)


def left_operand(rows):
    high, low = halves(rows)
    return jnp.concatenate([high, high, low], 0).T


def right_operand(refs):
    high, low = halves(jnp.concatenate([ref[...] for ref in refs], 0))
    return jnp.concatenate([high, low, high], 0)


def cost(flops, moved):
    return pl.CostEstimate(flops=flops, bytes_accessed=moved, transcendentals=0)


def stacked(blocks):
    rows, columns = blocks[0].shape

    def kernel(*refs):
        for i, ref in enumerate(refs[:-1]):
            refs[-1][rows * i : rows * (i + 1), :] = ref[...]

    return pl.pallas_call(
        kernel,
        out_shape=jax.ShapeDtypeStruct((rows * len(blocks), columns), blocks[0].dtype),
        compiler_params=pltpu.CompilerParams(vmem_limit_bytes=8 << 20),
        cost_estimate=cost(LONG, 8 * rows * columns * len(blocks)),
        name="stacked",
    )(*blocks)


def prepare(rotation, levels, cores, sources):
    width = rotation.shape[0] // levels
    piece = width // cores
    columns = rotation.shape[1]

    def kernel(rotation_ref, early_ref, late_ref):
        z = lax.axis_index("bands")

        def moved(level, offsets):
            even, odd = offsets
            return lax.rem(level + jnp.where(lax.rem(level, 2) == 0, even, odd) + levels, levels)

        def rows(part):
            found = []
            for source in part:
                holder = moved(z, source)
                for offsets in HELD:
                    level = moved(holder, offsets)
                    for core in range(cores):
                        at = pl.multiple_of((core * levels + level) * piece, piece)
                        found.append(rotation_ref[pl.ds(at, piece), :])
            return jnp.concatenate(found, 0)

        early_ref[...] = left_operand(rows(sources[0]))
        late_ref[...] = left_operand(rows(sources[1]))

    return pl.pallas_call(
        kernel,
        out_shape=[
            jax.ShapeDtypeStruct((columns, 3 * len(part) * len(HELD) * width), jnp.bfloat16) for part in sources
        ],
        compiler_params=pltpu.CompilerParams(vmem_limit_bytes=8 << 20),
        cost_estimate=cost(0, 5 * rotation.size * 4),
        name="prepare",
    )(rotation)


def add_part(left, total, parts):
    def kernel(left_ref, total_ref, *refs):
        refs[-1][...] = total_ref[...] + jnp.dot(
            left_ref[...], right_operand(refs[:-1]), preferred_element_type=jnp.float32
        )

    return pl.pallas_call(
        kernel,
        out_shape=jax.ShapeDtypeStruct(total.shape, jnp.float32),
        compiler_params=pltpu.CompilerParams(vmem_limit_bytes=20 << 20),
        cost_estimate=cost(2 * left.size * total.shape[1], 8 * total.size),
        name="add_part",
    )(left, total, *parts)


def add_last(left, total, parts):
    rows, columns = total.shape
    tiles = [(at, min(TILE, rows - at)) for at in range(0, rows, TILE)]

    def kernel(left_ref, total_ref, *refs):
        out_ref, held, sems = refs[-3:]
        right = right_operand(refs[:-3])
        stores = []
        for i, (at, size) in enumerate(tiles):
            held[at : at + size, :] = total_ref[at : at + size, :] + jnp.dot(
                left_ref[at : at + size, :], right, preferred_element_type=jnp.float32
            )
            stores.append(pltpu.make_async_copy(held.at[pl.ds(at, size)], out_ref.at[pl.ds(at, size)], sems.at[i]))
            stores[-1].start()
        for store in stores:
            store.wait()

    whole = pl.BlockSpec(memory_space=pltpu.VMEM)
    return pl.pallas_call(
        kernel,
        out_shape=jax.ShapeDtypeStruct(total.shape, jnp.float32),
        in_specs=[whole] * (2 + len(parts)),
        out_specs=pl.BlockSpec(memory_space=pl.ANY),
        scratch_shapes=[pltpu.VMEM((rows, columns), jnp.float32), pltpu.SemaphoreType.DMA((len(tiles),))],
        compiler_params=pltpu.CompilerParams(vmem_limit_bytes=20 << 20),
        cost_estimate=cost(2 * left.size * columns, 8 * total.size),
        name="add_last",
    )(left, total, *parts)


def solution(mesh):
    levels, planes = mesh.shape["bands"], mesh.shape["rows"]
    cores = 2
    chips = planes // cores
    same_core = [[cores * chip + core for chip in range(chips)] for core in range(cores)]
    same_chip = [[cores * chip + core for core in range(cores)] for chip in range(chips)]

    def fetched(block, offsets):
        pairs = [
            (i * levels + (z + offsets[z % 2]) % levels, i * levels + z) for i in range(planes) for z in range(levels)
        ]
        return lax.ppermute(block, ("rows", "bands"), pairs)

    def local(psi_panels, rotation, accumulated):
        copies = jnp.broadcast_to(rotation[None], (chips,) + rotation.shape)
        spread = lax.all_to_all(copies, "rows", 0, 0, axis_index_groups=same_core)
        spread = spread.reshape(-1, rotation.shape[1])
        pairs = [[z, (z + PAIR) % levels] for z in range(1, levels, 2)]
        couple = lax.all_gather(psi_panels.T, "bands", axis=0, tiled=True, axis_index_groups=pairs)
        own = stacked([couple, fetched(couple, HOP)])
        below, across, above = [fetched(own, offsets) for offsets in FROM[1:]]
        rot_whole = lax.all_gather(spread, "rows", axis=0, tiled=True, axis_index_groups=same_chip)
        early, late = prepare(rot_whole, levels, cores, (FROM[:3], FROM[3:]))
        total = add_part(early, accumulated.T, (own, below, across))
        return add_last(late, total, (above,)).T

    spec = P("rows", "bands")
    return jax.shard_map(local, mesh=mesh, in_specs=(spec, spec, spec), out_specs=spec, check_vma=False)
```
